32 devices in a mesh: rep: 2 (over y), clu: 8 (over z, x), sub: 2 (over core).
Axes of the slice: x: 2, y: 2, z: 4, core: 2. Of those that a mesh axis runs over, the one named last changes fastest.
Arguments:
- electronegativity: float32 [128, 256], P(('rep', 'clu'), 'sub'), parts along dimension 0, may hold values from -6 to 6
- mm_potential: float32 [128, 256], P(('rep', 'clu'), 'sub'), parts along dimension 0, may hold values from -12 to 12
- hardness: float32 [128, 256], P(('rep', 'clu'), 'sub'), parts along dimension 0, may hold values from 4 to 10
- near_blocks: bfloat16 [128, 3, 256, 256], P(('rep', 'clu'), None, 'sub'), parts along dimension 0, as said below
- near_source: int32 [128, 3], P(('rep', 'clu')), parts along dimension 0, may hold values from 0 to 63, as said below
- basis_in: bfloat16 [128, 32, 256], P(('rep', 'clu'), None, 'sub'), parts along dimension 0, may hold values from -0.375 to 0.375
- far_coupling: bfloat16 [16, 8, 4, 1024], P(('rep', 'clu')), parts along dimension 0
- far_source: int32 [16, 8, 4], P(('rep', 'clu')), parts along dimension 0, may hold values from 0 to 7, as said below
- far_target: int32 [16, 8, 4], P(('rep', 'clu')), parts along dimension 0, may hold values from 0 to 7
- far_count: int32 [16, 8], P(('rep', 'clu')), parts along dimension 0, may hold values from 0 to 4, as said below
Outputs:
- charges: float32 [128, 256], P(('rep', 'clu'), 'sub'), parts along dimension 0
- residual: float32 [128, 256], P(('rep', 'clu'), 'sub'), parts along dimension 0
The draws below stay inside these ranges and needn't reach their ends.
There are 2 independent parts, one for each index of `rep`. The reference program is written for one: setup_inputs(seed, part) draws one part's arguments, and reference() takes and returns one part's arrays. A program takes and returns all parts, laid end to end along the dimension named above; each array names one. Nothing has to cross between parts.
Inputs may be any that keep to these rules, and one draw needn't show every extreme that they name: `near_source`: entry 0 of each cluster's list is the cluster itself; the other two entries are, in either order, the clusters 8 above and 8 below it, replaced by the cluster itself where that one does not exist. `near_blocks`: the near operator is symmetric: the block of cluster c for source s is the transpose of the block of s for source c, and the sum of a cluster's blocks whose source is itself is symmetric. Slots at or past the count are unused; far_count is symmetric, zero from an owner to itself, and every row of receiving owners has some sending owner using all 4 slots. `far_source`: slot k from s to d is the mirror of slot k from d to s: source and target are swapped and the coupling matrix is transposed.
All inputs are finite; a program needn't handle non-finite values.
Results may differ from the reference program's by a relative error of at most 0.00055.
Values sent between devices are 32-bit elements; how exact they have to be, the bound alone decides.
A program may use at most 64 MiB of HBM per device.

```python
import math
import jax
import jax.numpy as jnp
from jax import lax

CL_DEV = 8
B = 256
R = 32
NEAR = 3
CAP = 4
ITERS = 3
OWNERS = 8
CLUSTERS = 64


def near_order(key):
    return jax.random.randint(jax.random.fold_in(key, 21), (CLUSTERS,), 0, 2).astype(jnp.int32)


def far_parts(key):
    key = jax.random.fold_in(key, 31)
    key_src, key_tgt, key_cpl, key_cnt, key_shift = jax.random.split(key, 5)
    raw_src = jax.random.randint(key_src, (OWNERS, OWNERS, CAP), 0, CL_DEV).astype(jnp.int32)
    raw_tgt = jax.random.randint(key_tgt, (OWNERS, OWNERS, CAP), 0, CL_DEV).astype(jnp.int32)
    recv = jnp.arange(OWNERS, dtype=jnp.int32)[:, None]
    send = jnp.arange(OWNERS, dtype=jnp.int32)[None, :]
    lower = recv > send
    sources = jnp.where(lower[..., None], jnp.swapaxes(raw_tgt, 0, 1), raw_src)
    targets = jnp.where(lower[..., None], jnp.swapaxes(raw_src, 0, 1), raw_tgt)
    scale = (R * OWNERS * CAP / CL_DEV) ** (-0.5)
    raw_cpl = jax.random.normal(key_cpl, (OWNERS, OWNERS, CAP, R, R), jnp.float32) * scale
    mirrored = jnp.swapaxes(jnp.swapaxes(raw_cpl, 0, 1), 3, 4)
    couplings = jnp.where(lower[..., None, None, None], mirrored, raw_cpl).reshape(OWNERS, OWNERS, CAP, R * R)
    upper = jax.random.randint(key_cnt, (OWNERS, OWNERS), 0, CAP + 1).astype(jnp.int32)
    counts = jnp.where(recv < send, upper, upper.T)
    shift = jax.random.randint(key_shift, (), 1, OWNERS).astype(jnp.int32)
    gap = (send - recv) % OWNERS
    full = (gap == shift) | ((OWNERS - gap) % OWNERS == shift)
    counts = jnp.where(full, CAP, counts)
    counts = jnp.where(recv == send, 0, counts).astype(jnp.int32)
    return (sources, targets, couplings, counts)


def draw_near_source(key, part):
    order = near_order(key)
    positions = jnp.arange(CLUSTERS, dtype=jnp.int32)
    above = jnp.where(positions + CL_DEV < CLUSTERS, positions + CL_DEV, positions)
    below = jnp.where(positions >= CL_DEV, positions - CL_DEV, positions)
    first = jnp.where(order == 1, below, above)
    second = jnp.where(order == 1, above, below)
    return jnp.stack([positions, first, second], axis=1).astype(jnp.int32)


def draw_near_blocks(key, part):
    order = near_order(key)
    key = jax.random.fold_in(key, 14)
    key_pair, key_self, key_edge = jax.random.split(key, 3)
    scale = (4.0 * B * NEAR) ** (-0.5)
    pairs = jax.random.normal(key_pair, (CLUSTERS, B, B), jnp.float32) * scale
    selfs = jax.random.normal(key_self, (CLUSTERS, B, B), jnp.float32) * scale
    edges = jax.random.normal(key_edge, (CLUSTERS, B, B), jnp.float32) * scale
    selfs = (selfs + jnp.swapaxes(selfs, 1, 2)) * 0.7071
    edges = (edges + jnp.swapaxes(edges, 1, 2)) * 0.7071
    positions = jnp.arange(CLUSTERS, dtype=jnp.int32)[:, None, None]
    above_block = jnp.where(positions + CL_DEV < CLUSTERS, pairs, edges)
    below_block = jnp.where(positions >= CL_DEV, jnp.swapaxes(jnp.roll(pairs, CL_DEV, axis=0), 1, 2), edges)
    swapped = (order == 1)[:, None, None]
    first = jnp.where(swapped, below_block, above_block)
    second = jnp.where(swapped, above_block, below_block)
    return jnp.stack([selfs, first, second], axis=1).astype(jnp.bfloat16)


def draw_far_source(key, part):
    return far_parts(key)[0]


def draw_far_target(key, part):
    return far_parts(key)[1]


def draw_far_coupling(key, part):
    return far_parts(key)[2].astype(jnp.bfloat16)


def draw_far_count(key, part):
    return far_parts(key)[3]


def draw_mm_potential(key, part):
    key = jax.random.fold_in(key, 13)
    key_scale, key_rough = jax.random.split(key)
    rising = 0.5 + jnp.arange(CLUSTERS, dtype=jnp.float32)[:, None] / CLUSTERS
    spread = jnp.exp(jax.random.uniform(key_scale, (CLUSTERS, 1), minval=-1.15, maxval=1.15))
    rough = jax.random.normal(key_rough, (CLUSTERS, B))
    return jnp.clip(rough * rising * spread, -12.0, 12.0).astype(jnp.float32)


def levels(own_key, shape, pieces, least, largest):
    gain = 1.0
    for position, parts in pieces:
        draws = jax.random.uniform(jax.random.fold_in(jax.random.fold_in(own_key, 6), position), (parts,), jnp.float32, least / len(pieces), largest / len(pieces))
        gain = gain * jnp.repeat(jnp.exp(draws), shape[position] // parts).reshape((-1,) + (1,) * (len(shape) - 1 - position))
    return gain


def normal_values(key, dims, width, limit, shards=(), held_as=jnp.bfloat16):
    array = jax.random.normal(key, dims, jnp.float32) * width
    if len(shards) > 0:
        array = levels(key, dims, shards, -0.22, 0.18) * array
    return jnp.clip(array, min=-limit, max=limit).astype(held_as)


def setup_inputs(seed: int = 0, part: int = 0) -> dict:
    keys = jax.random.split(jax.random.key(seed), 11)
    part_splits = jax.random.split(jax.random.fold_in(keys[10], part), 11)
    electronegativity = normal_values(part_splits[0], (CLUSTERS, B), 1.0, 6.0, ((0, 8), (1, 2)), jnp.float32)
    mm_potential = draw_mm_potential(jax.random.fold_in(jax.random.fold_in(keys[10], part), 71), part)
    hardness = jnp.clip(jnp.exp(math.log(10.0) - 0.916290732 * jax.random.uniform(part_splits[2], (CLUSTERS, B), jnp.float32) ** levels(part_splits[2], (CLUSTERS, B), ((0, 8), (1, 2)), -0.2, 0.2)), 4.0, 10.0)
    near_blocks = draw_near_blocks(jax.random.fold_in(jax.random.fold_in(keys[10], part), 71), part)
    near_source = draw_near_source(jax.random.fold_in(jax.random.fold_in(keys[10], part), 71), part)
    basis_in = normal_values(part_splits[5], (CLUSTERS, R, B), B ** -0.5, 0.375, ((0, 8), (2, 2)))
    far_coupling = draw_far_coupling(jax.random.fold_in(jax.random.fold_in(keys[10], part), 71), part)
    far_source = draw_far_source(jax.random.fold_in(jax.random.fold_in(keys[10], part), 71), part)
    far_target = draw_far_target(jax.random.fold_in(jax.random.fold_in(keys[10], part), 71), part)
    far_count = draw_far_count(jax.random.fold_in(jax.random.fold_in(keys[10], part), 71), part)
    return {"electronegativity": electronegativity, "mm_potential": mm_potential, "hardness": hardness, "near_blocks": near_blocks, "near_source": near_source, "basis_in": basis_in, "far_coupling": far_coupling, "far_source": far_source, "far_target": far_target, "far_count": far_count}


HIGHEST = lax.Precision.HIGHEST


def reference(electronegativity, mm_potential, hardness, near_blocks, near_source, basis_in, far_coupling, far_source, far_target, far_count):
    coupling = far_coupling.astype(jnp.float32).reshape(OWNERS, OWNERS, CAP, R, R)
    bases_in = basis_in.astype(jnp.float32)
    owner_ids = jnp.arange(OWNERS, dtype=jnp.int32)
    source_ids = owner_ids[None, :, None] * CL_DEV + far_source
    target_ids = (owner_ids[:, None, None] * CL_DEV + far_target).reshape(-1).astype(jnp.int32)
    live_slots = (jnp.arange(CAP, dtype=jnp.int32)[None, None, :] < far_count[:, :, None]).astype(jnp.float32)
    grouped_blocks = near_blocks.reshape(OWNERS, CL_DEV, NEAR, B, B)
    grouped_source = near_source.reshape(OWNERS, CL_DEV, NEAR)

    def apply_operator(field):
        def near_group(pair):
            blocks, sources = pair
            picked = field[sources]
            return jnp.einsum("cnab,cnb->ca", blocks.astype(jnp.float32), picked, precision=HIGHEST)

        near_term = lax.map(near_group, (grouped_blocks, grouped_source)).reshape(CLUSTERS, B)
        coeffs = jnp.einsum("crb,cb->cr", bases_in, field, precision=HIGHEST)
        slots = coeffs[source_ids]
        moved_terms = jnp.einsum("dskab,dskb->dska", coupling, slots, precision=HIGHEST) * live_slots[..., None]
        target_sums = jax.ops.segment_sum(moved_terms.reshape(-1, R), target_ids, num_segments=CLUSTERS)
        far_term = jnp.einsum("ca,cab->cb", target_sums, bases_in, precision=HIGHEST)
        return hardness * field + near_term + far_term

    right = -(electronegativity + mm_potential)
    charges = jnp.zeros_like(right)
    residual = right
    direction = right
    norm_now = jnp.sum(residual * residual)
    for iteration in range(ITERS):
        product_vec = apply_operator(direction)
        step_size = norm_now / jnp.sum(direction * product_vec)
        charges = charges + step_size * direction
        residual = residual - step_size * product_vec
        norm_next = jnp.sum(residual * residual)
        direction = residual + (norm_next / norm_now) * direction
        norm_now = norm_next
    return charges, residual
```

```python
import functools

import jax
import jax.numpy as jnp
from jax import lax
from jax.experimental import pallas as pl
from jax.experimental.pallas import tpu as pltpu
from jax.sharding import PartitionSpec as P

ITERS = 3
MESH = pl.DeviceIdType.MESH
F32 = jnp.float32
BF16 = jnp.bfloat16
SELF, ABOVE, BELOW = 0, 1, 2


def each(first, count, body):
    if count - first <= 8:
        for i in range(first, count):
            body(i)
    else:
        lax.fori_loop(first, count, lambda i, _: (body(i), 0)[1], 0)


def halves(x):
    high = x.astype(BF16)
    low = (x - high.astype(F32)).astype(BF16)
    return high, low


def contract(a, b, dims):
    return lax.dot_general(a, b, (dims, ((), ())), preferred_element_type=F32)


def kernel(
    owners,
    electro,
    potential,
    hardness_ref,
    near_hbm,
    near_source,
    basis,
    coupling,
    target,
    count,
    charges_out,
    residual_out,
    near,
    picked_basis,
    expand,
    mask,
    fields,
    outbox,
    inbox,
    load_sem,
    field_send,
    field_recv,
    slab_send,
    slab_recv,
):
    clusters, atoms = hardness_ref.shape
    slots = target.shape[2]
    rank = basis.shape[1]
    width = slots * rank
    group = 8
    groups = owners // group
    span = group * width
    peers = 2 * owners - 1
    clu = lax.axis_index("clu")
    sub = lax.axis_index("sub")
    mine = 2 * clu + sub

    def to_peers(act):
        def owner_step(o):
            d = lax.rem(clu + o, owners)
            act(d, 0)
            act(d, 1)

        act(clu, 1 - sub)
        each(1, owners, owner_step)

    barrier = pltpu.get_barrier_semaphore()
    to_peers(
        lambda d, t: pl.semaphore_signal(
            barrier, inc=1, device_id={"clu": d, "sub": t}, device_id_type=MESH
        )
    )
    load = pltpu.make_async_copy(near_hbm, near, load_sem)
    load.start()

    row8 = lax.broadcasted_iota(jnp.int32, (clusters, 128), 0)
    slot_of_lane = lax.broadcasted_iota(jnp.int32, (clusters, width), 1) // rank

    def prepare(s):
        wanted = jnp.full((clusters, width), -1, jnp.int32)
        for k in range(slots):
            t = target[0, s, k]
            picked_basis[pl.ds((s * slots + k) * rank, rank), :] = basis[t]
            wanted = jnp.where(slot_of_lane == k, t, wanted)
        hit = (wanted == lax.broadcasted_iota(jnp.int32, (clusters, width), 0)) & (
            slot_of_lane < count[0, s]
        )
        mask[s] = jnp.where(hit, 1.0, 0.0)

    each(0, owners, prepare)

    def send_field(rnd, v):
        fields[rnd, SELF, sub] = v
        source = fields.at[rnd, SELF, sub]

        def copy(kind, d, t):
            pltpu.make_async_remote_copy(
                src_ref=source,
                dst_ref=fields.at[rnd, kind, sub],
                send_sem=field_send.at[rnd, kind],
                recv_sem=field_recv.at[rnd, kind],
                device_id={"clu": d, "sub": t},
                device_id_type=MESH,
            ).start()

        copy(SELF, clu, 1 - sub)

        @pl.when(clu < owners - 1)
        def _():
            copy(BELOW, clu + 1, 0)
            copy(BELOW, clu + 1, 1)

        @pl.when(clu > 0)
        def _():
            copy(ABOVE, clu - 1, 0)
            copy(ABOVE, clu - 1, 1)

    def send_slabs(rnd, sums):
        def copy(d, t):
            pltpu.make_async_remote_copy(
                src_ref=outbox.at[rnd, d],
                dst_ref=inbox.at[rnd, mine],
                send_sem=slab_send.at[rnd],
                recv_sem=slab_recv.at[rnd],
                device_id={"clu": d, "sub": t},
                device_id_type=MESH,
            ).start()

        to_peers(copy)
        inbox[rnd, mine] = sums

    def send_far(rnd, v, sums):
        parts = jnp.concatenate(halves(v), axis=0)

        def group_step(g):
            wide = contract(
                parts, picked_basis[pl.ds(pl.multiple_of(g * span, span), span), :], ((1,), (1,))
            )
            for j in range(group):
                piece = wide[:, j * width : (j + 1) * width]
                piece = (piece[:clusters] + piece[clusters:]) * mask[g * group + j]
                line = jnp.sum(piece, axis=0, keepdims=True)
                outbox[rnd, g * group + j] = jnp.where(row8 == 0, line, sums)

        each(0, groups, group_step)
        send_slabs(rnd, jnp.where(row8 == 0, 0.0, sums))

    def send_sums(rnd, sums):
        each(0, owners, lambda d: outbox.__setitem__((rnd, d), sums))
        send_slabs(rnd, sums)

    def wait_all(ref, sem):
        pltpu.make_async_copy(ref, ref, sem).wait()

    def near_term(rnd):
        wait_all(fields.at[rnd, SELF, 0], field_recv.at[rnd, SELF])

        @pl.when(clu < owners - 1)
        def _():
            wait_all(fields.at[rnd, ABOVE], field_recv.at[rnd, ABOVE])

        @pl.when(clu > 0)
        def _():
            wait_all(fields.at[rnd, BELOW], field_recv.at[rnd, BELOW])

        def whole(kind):
            return jnp.concatenate([fields[rnd, kind, 0], fields[rnd, kind, 1]], axis=1)

        own, above, below = (whole(SELF), whole(ABOVE), whole(BELOW))
        here = clu * clusters + lax.broadcasted_iota(jnp.int32, (clusters, 1), 0)
        inputs = []
        for n in range(near.shape[1]):
            if n == 0:
                value = own
            else:
                origin = near_source[:, n : n + 1]
                value = jnp.where(
                    origin == here + clusters,
                    above,
                    jnp.where(origin == here - clusters, below, own),
                )
            inputs.append(jnp.concatenate(halves(value), axis=0))
        owner_row = lax.broadcasted_iota(jnp.int32, inputs[0].shape, 0) % clusters
        total = None
        blocks = [(c, n) for c in range(clusters) for n in range(near.shape[1])]
        for first, second in zip(blocks[::2], blocks[1::2]):
            left = jnp.concatenate(
                [
                    jnp.where(owner_row == c, inputs[n], jnp.zeros_like(inputs[n]))
                    for c, n in (first, second)
                ],
                axis=0,
            )
            right = jnp.concatenate([near[c, n] for c, n in (first, second)], axis=0)
            product = contract(left, right, ((1,), (1,)))
            total = product if total is None else total + product
        size = 2 * clusters
        first, second = (total[:size, :atoms], total[size:, atoms:])
        both = first + second
        return both[:clusters] + both[clusters:]

    def receive(rnd):
        wait_all(inbox.at[rnd, pl.ds(0, peers)], slab_recv.at[rnd])

    def far_term(rnd):
        def group_step(g):
            lefts = []
            for j in range(group):
                s = g * group + j
                line = inbox[rnd, 2 * s, 0:1, :] + inbox[rnd, 2 * s + 1, 0:1, :]
                lefts.append(line * mask[s])
            left = jnp.concatenate(lefts, axis=1)
            left = jnp.concatenate(halves(left), axis=0)
            right = expand[pl.ds(pl.multiple_of(g * span, span), span), :]
            out = contract(left, right, ((1,), (0,)))
            out = out[:clusters] + out[clusters:]
            return out[:, :atoms] + out[:, atoms:]

        if groups == 1:
            return group_step(0)
        return lax.fori_loop(
            0, groups, lambda g, acc: acc + group_step(g), jnp.zeros((clusters, atoms), F32)
        )

    def totals(rnd):
        if owners <= 8:
            values = [inbox[rnd, i] for i in range(2 * owners)]
            while len(values) > 1:
                values = [a + b for a, b in zip(values[::2], values[1::2])]
            all_sums = values[0]
        else:
            all_sums = lax.fori_loop(
                0, 2 * owners, lambda i, acc: acc + inbox[rnd, i], jnp.zeros((8, 128), F32)
            )
        lane_sum = jnp.sum(all_sums, axis=1, keepdims=True)
        return [lane_sum[i : i + 1, :] for i in range(1, 5)]

    def pack(*pairs):
        out = jnp.zeros((8, 128), F32)
        for i, (a, b) in enumerate(pairs):
            out = jnp.where(row8 == i + 1, jnp.sum(a * b, axis=0, keepdims=True), out)
        return out

    def build_expand():
        row = lax.broadcasted_iota(jnp.int32, (width, width), 0)
        lane = lax.broadcasted_iota(jnp.int32, (width, width), 1)
        spread = jnp.where(row % rank == lane % rank, 1.0, 0.0).astype(BF16)
        per_chunk = width // rank
        same = row // rank == lane // rank

        def step(s):
            lines = coupling[0, s].astype(F32)
            folded = jnp.zeros((width, width), F32)
            for j in range(rank * rank // width):
                chunk = lines[:, j * width : (j + 1) * width]
                tall = jnp.broadcast_to(chunk[:, None, :], (slots, rank, width)).reshape(
                    width, width
                )
                folded = jnp.where(row % rank == lane // rank + j * per_chunk, tall, folded)
            tiled = contract(folded.astype(BF16), spread, ((1,), (0,)))
            diagonal = jnp.where(same, tiled, 0.0).astype(BF16)
            place = pl.ds(pl.multiple_of(s * width, width), width)
            high, low = halves(contract(diagonal, picked_basis[place, :], ((0,), (0,))))
            expand[place, 0:atoms] = high
            expand[place, atoms : 2 * atoms] = low

        each(0, owners, step)

    hardness = hardness_ref[...]
    r = -(electro[...] + potential[...])
    x = jnp.zeros_like(r)
    empty = jnp.zeros((8, 128), F32)
    pl.semaphore_wait(barrier, peers)

    send_field(0, r)
    send_far(0, r, empty)
    build_expand()
    load.wait()
    w = hardness * r + near_term(0)
    receive(0)
    w = w + far_term(0)

    p, s, z, rr, curvature, step = (None,) * 6
    for i in range(ITERS):
        rnd = i + 1
        if i == 0:
            sums = pack((r, r), (r, w))
        else:
            sums = pack((r, r), (r, w), (r, s), (p, w))
        last = i == ITERS - 1
        if last:
            send_sums(rnd, sums)
            receive(rnd)
        else:
            send_field(rnd, w)
            send_far(rnd, w, sums)
            q = hardness * w + near_term(rnd)
            receive(rnd)
        new, rw, rs, pw = totals(rnd)
        if not last:
            q = q + far_term(rnd)
        if i == 0:
            curvature = rw
            p, s = (r, w)
            z = q
        else:
            ratio = new / rr
            curvature = rw + ratio * (rs + pw) + ratio * ratio * curvature
            p = r + ratio * p
            s = w + ratio * s
            if not last:
                z = q + ratio * z
        rr = new
        step = rr / curvature
        x = x + step * p
        r = r - step * s
        if not last:
            w = w - step * z
    charges_out[...] = x
    residual_out[...] = r

    for rnd in range(ITERS):
        wait_all(fields.at[rnd, SELF, 0], field_send.at[rnd, SELF])

        @pl.when(clu < owners - 1)
        def _():
            wait_all(fields.at[rnd, BELOW], field_send.at[rnd, BELOW])

        @pl.when(clu > 0)
        def _():
            wait_all(fields.at[rnd, ABOVE], field_send.at[rnd, ABOVE])

    for rnd in range(ITERS + 1):
        wait_all(inbox.at[rnd, pl.ds(0, peers)], slab_send.at[rnd])


def shards(
    electronegativity,
    mm_potential,
    hardness,
    near_blocks,
    near_source,
    basis_in,
    far_coupling,
    far_source,
    far_target,
    far_count,
):
    clusters, atoms = hardness.shape
    owners = far_coupling.shape[1]
    width = far_coupling.shape[2] * basis_in.shape[1]
    vmem = pl.BlockSpec(memory_space=pltpu.VMEM)
    smem = pl.BlockSpec(memory_space=pltpu.SMEM)
    whole = pl.BlockSpec(memory_space=pl.ANY)
    rounds = ITERS + 1
    return pl.pallas_call(
        functools.partial(kernel, owners),
        out_shape=(jax.ShapeDtypeStruct(hardness.shape, F32),) * 2,
        in_specs=[vmem, vmem, vmem, whole, vmem, vmem, vmem, smem, smem],
        out_specs=(vmem, vmem),
        scratch_shapes=[
            pltpu.VMEM(near_blocks.shape, BF16),
            pltpu.VMEM((owners * width, atoms), BF16),
            pltpu.VMEM((owners * width, 2 * atoms), BF16),
            pltpu.VMEM((owners, clusters, width), F32),
            pltpu.VMEM((ITERS, 3, 2, clusters, atoms), F32),
            pltpu.VMEM((rounds, owners, 8, 128), F32),
            pltpu.VMEM((rounds, 2 * owners, 8, 128), F32),
            pltpu.SemaphoreType.DMA,
            pltpu.SemaphoreType.DMA((ITERS, 3)),
            pltpu.SemaphoreType.DMA((ITERS, 3)),
            pltpu.SemaphoreType.DMA((rounds,)),
            pltpu.SemaphoreType.DMA((rounds,)),
        ],
        compiler_params=pltpu.CompilerParams(
            collective_id=0, has_side_effects=True, vmem_limit_bytes=50 * 2**20
        ),
    )(
        electronegativity,
        mm_potential,
        hardness,
        near_blocks,
        near_source,
        basis_in,
        far_coupling,
        far_target,
        far_count,
    )


def solution(mesh):
    placed = (
        P(("rep", "clu"), "sub"),
        P(("rep", "clu"), "sub"),
        P(("rep", "clu"), "sub"),
        P(("rep", "clu"), None, "sub", None),
        P(("rep", "clu"), None),
        P(("rep", "clu"), None, "sub"),
        P(("rep", "clu"), None, None, None),
        P(("rep", "clu"), None, None),
        P(("rep", "clu"), None, None),
        P(("rep", "clu"), None),
    )
    return jax.shard_map(
        shards,
        mesh=mesh,
        in_specs=placed,
        out_specs=(P(("rep", "clu"), "sub"), P(("rep", "clu"), "sub")),
        check_vma=False,
    )
```

```python
import functools

import jax
import jax.numpy as jnp
from jax import lax
from jax.experimental import pallas as pl
from jax.experimental.pallas import tpu as pltpu
from jax.sharding import PartitionSpec as P

ITERS = 3
MESH = pl.DeviceIdType.MESH
F32 = jnp.float32
BF16 = jnp.bfloat16
SELF, ABOVE, BELOW = 0, 1, 2


def each(first, count, body):
    if count - first <= 8:
        for i in range(first, count):
            body(i)
    else:
        lax.fori_loop(first, count, lambda i, _: (body(i), 0)[1], 0)


def halves(x):
    high = x.astype(BF16)
    low = (x - high.astype(F32)).astype(BF16)
    return high, low


def contract(a, b, dims):
    return lax.dot_general(a, b, (dims, ((), ())), preferred_element_type=F32)


def kernel(
    owners,
    *refs,
):
    arguments, refs = (refs[:9], refs[9:])
    charges_out, residual_out = refs[:2]
    held, refs = (refs[2:11], refs[11:])
    target, count, basis, electro, potential, coupling, near, near_source, hardness_ref = held
    (
        picked_basis,
        expand,
        mask,
        fields,
        outbox,
        inbox,
        load_sem,
        field_send,
        field_recv,
        slab_send,
        slab_recv,
    ) = refs
    loads = [
        pltpu.make_async_copy(source, place, load_sem.at[i])
        for i, (source, place) in enumerate(zip(arguments, held))
    ]
    clusters, atoms = hardness_ref.shape
    slots = target.shape[1]
    rank = basis.shape[1]
    width = slots * rank
    group = 8
    groups = owners // group
    span = group * width
    peers = 2 * owners - 1
    clu = lax.axis_index("clu")
    sub = lax.axis_index("sub")
    mine = 2 * clu + sub

    def to_peers(act):
        def owner_step(o):
            d = lax.rem(clu + o, owners)
            act(d, 0)
            act(d, 1)

        act(clu, 1 - sub)
        each(1, owners, owner_step)

    for copy in loads:
        copy.start()
    barrier = pltpu.get_barrier_semaphore()
    to_peers(
        lambda d, t: pl.semaphore_signal(
            barrier, inc=1, device_id={"clu": d, "sub": t}, device_id_type=MESH
        )
    )

    row8 = lax.broadcasted_iota(jnp.int32, (clusters, 128), 0)
    slot_of_lane = lax.broadcasted_iota(jnp.int32, (clusters, width), 1) // rank

    def prepare(s):
        wanted = jnp.full((clusters, width), -1, jnp.int32)
        for k in range(slots):
            t = target[0, k, s]
            picked_basis[pl.ds((s * slots + k) * rank, rank), :] = basis[t]
            wanted = jnp.where(slot_of_lane == k, t, wanted)
        hit = (wanted == lax.broadcasted_iota(jnp.int32, (clusters, width), 0)) & (
            slot_of_lane < count[0, s]
        )
        mask[s] = jnp.where(hit, 1.0, 0.0)

    for copy in loads[:3]:
        copy.wait()
    each(0, owners, prepare)

    def send_field(rnd, v):
        fields[rnd, SELF, sub] = v
        source = fields.at[rnd, SELF, sub]

        def copy(kind, d, t):
            pltpu.make_async_remote_copy(
                src_ref=source,
                dst_ref=fields.at[rnd, kind, sub],
                send_sem=field_send.at[rnd, kind],
                recv_sem=field_recv.at[rnd, kind],
                device_id={"clu": d, "sub": t},
                device_id_type=MESH,
            ).start()

        copy(SELF, clu, 1 - sub)

        @pl.when(clu < owners - 1)
        def _():
            copy(BELOW, clu + 1, 0)
            copy(BELOW, clu + 1, 1)

        @pl.when(clu > 0)
        def _():
            copy(ABOVE, clu - 1, 0)
            copy(ABOVE, clu - 1, 1)

    def send_slabs(rnd, sums):
        def copy(d, t):
            pltpu.make_async_remote_copy(
                src_ref=outbox.at[rnd, d],
                dst_ref=inbox.at[rnd, mine],
                send_sem=slab_send.at[rnd],
                recv_sem=slab_recv.at[rnd],
                device_id={"clu": d, "sub": t},
                device_id_type=MESH,
            ).start()

        to_peers(copy)
        inbox[rnd, mine] = sums

    def send_far(rnd, v, sums):
        parts = jnp.concatenate(halves(v), axis=0)

        def group_step(g):
            wide = contract(
                parts, picked_basis[pl.ds(pl.multiple_of(g * span, span), span), :], ((1,), (1,))
            )
            for j in range(group):
                piece = wide[:, j * width : (j + 1) * width]
                piece = (piece[:clusters] + piece[clusters:]) * mask[g * group + j]
                line = jnp.sum(piece, axis=0, keepdims=True)
                outbox[rnd, g * group + j] = jnp.where(row8 == 0, line, sums)

        each(0, groups, group_step)
        send_slabs(rnd, jnp.where(row8 == 0, 0.0, sums))

    def send_sums(rnd, sums):
        each(0, owners, lambda d: outbox.__setitem__((rnd, d), sums))
        send_slabs(rnd, sums)

    def wait_all(ref, sem):
        pltpu.make_async_copy(ref, ref, sem).wait()

    def near_term(rnd):
        wait_all(fields.at[rnd, SELF, 0], field_recv.at[rnd, SELF])

        @pl.when(clu < owners - 1)
        def _():
            wait_all(fields.at[rnd, ABOVE], field_recv.at[rnd, ABOVE])

        @pl.when(clu > 0)
        def _():
            wait_all(fields.at[rnd, BELOW], field_recv.at[rnd, BELOW])

        def whole(kind):
            return jnp.concatenate([fields[rnd, kind, 0], fields[rnd, kind, 1]], axis=1)

        own, above, below = (whole(SELF), whole(ABOVE), whole(BELOW))
        inputs = []
        for n in range(near.shape[1]):
            if n == 0:
                value = own
            else:
                origin = origins[n]
                value = jnp.where(
                    origin == here + clusters,
                    above,
                    jnp.where(origin == here - clusters, below, own),
                )
            inputs.append(jnp.concatenate(halves(value), axis=0))
        owner_row = lax.broadcasted_iota(jnp.int32, inputs[0].shape, 0) % clusters
        total = None
        blocks = [(c, n) for c in range(clusters) for n in range(near.shape[1])]
        for first, second in zip(blocks[::2], blocks[1::2]):
            left = jnp.concatenate(
                [
                    jnp.where(owner_row == c, inputs[n], jnp.zeros_like(inputs[n]))
                    for c, n in (first, second)
                ],
                axis=0,
            )
            right = jnp.concatenate([near[c, n] for c, n in (first, second)], axis=0)
            product = contract(left, right, ((1,), (1,)))
            total = product if total is None else total + product
        size = 2 * clusters
        first, second = (total[:size, :atoms], total[size:, atoms:])
        both = first + second
        return both[:clusters] + both[clusters:]

    def receive(rnd):
        wait_all(inbox.at[rnd, pl.ds(0, peers)], slab_recv.at[rnd])

    def far_term(rnd):
        def group_step(g):
            lefts = []
            for j in range(group):
                s = g * group + j
                line = inbox[rnd, 2 * s, 0:1, :] + inbox[rnd, 2 * s + 1, 0:1, :]
                lefts.append(line * mask[s])
            left = jnp.concatenate(lefts, axis=1)
            left = jnp.concatenate(halves(left), axis=0)
            right = expand[pl.ds(pl.multiple_of(g * span, span), span), :]
            out = contract(left, right, ((1,), (0,)))
            out = out[:clusters] + out[clusters:]
            return out[:, :atoms] + out[:, atoms:]

        if groups == 1:
            return group_step(0)
        return lax.fori_loop(
            0, groups, lambda g, acc: acc + group_step(g), jnp.zeros((clusters, atoms), F32)
        )

    def totals(rnd):
        if owners <= 8:
            values = [inbox[rnd, i] for i in range(2 * owners)]
            while len(values) > 1:
                values = [a + b for a, b in zip(values[::2], values[1::2])]
            all_sums = values[0]
        else:
            all_sums = lax.fori_loop(
                0, 2 * owners, lambda i, acc: acc + inbox[rnd, i], jnp.zeros((8, 128), F32)
            )
        lane_sum = jnp.sum(all_sums, axis=1, keepdims=True)
        return [lane_sum[i : i + 1, :] for i in range(1, 5)]

    def pack(*pairs):
        out = jnp.zeros((8, 128), F32)
        for i, (a, b) in enumerate(pairs):
            out = jnp.where(row8 == i + 1, jnp.sum(a * b, axis=0, keepdims=True), out)
        return out

    def build_expand():
        row = lax.broadcasted_iota(jnp.int32, (width, width), 0)
        lane = lax.broadcasted_iota(jnp.int32, (width, width), 1)
        spread = jnp.where(row % rank == lane % rank, 1.0, 0.0).astype(BF16)
        per_chunk = width // rank
        same = row // rank == lane // rank

        def step(s):
            lines = coupling[0, s].astype(F32)
            folded = jnp.zeros((width, width), F32)
            for j in range(rank * rank // width):
                chunk = lines[:, j * width : (j + 1) * width]
                tall = jnp.broadcast_to(chunk[:, None, :], (slots, rank, width)).reshape(
                    width, width
                )
                folded = jnp.where(row % rank == lane // rank + j * per_chunk, tall, folded)
            tiled = contract(folded.astype(BF16), spread, ((1,), (0,)))
            diagonal = jnp.where(same, tiled, 0.0).astype(BF16)
            place = pl.ds(pl.multiple_of(s * width, width), width)
            high, low = halves(contract(diagonal, picked_basis[place, :], ((0,), (0,))))
            expand[place, 0:atoms] = high
            expand[place, atoms : 2 * atoms] = low

        each(0, owners, step)

    for copy in loads[3:5]:
        copy.wait()
    r = -(electro[...] + potential[...])
    x = jnp.zeros_like(r)
    empty = jnp.zeros((8, 128), F32)
    pl.semaphore_wait(barrier, peers)

    send_field(0, r)
    send_far(0, r, empty)
    loads[5].wait()
    build_expand()
    for copy in loads[6:]:
        copy.wait()
    hardness = hardness_ref[...]
    here = clu * clusters + lax.broadcasted_iota(jnp.int32, (clusters, 2 * atoms), 0)
    origins = []
    for n in range(near.shape[1]):
        origin = here
        for c in range(clusters):
            origin = jnp.where(here == clu * clusters + c, near_source[n, c], origin)
        origins.append(origin)
    w = hardness * r + near_term(0)
    receive(0)
    w = w + far_term(0)

    p, s, z, rr, curvature, step = (None,) * 6
    for i in range(ITERS):
        rnd = i + 1
        if i == 0:
            sums = pack((r, r), (r, w))
        else:
            sums = pack((r, r), (r, w), (r, s), (p, w))
        last = i == ITERS - 1
        if last:
            send_sums(rnd, sums)
            receive(rnd)
        else:
            send_field(rnd, w)
            send_far(rnd, w, sums)
            q = hardness * w + near_term(rnd)
            receive(rnd)
        new, rw, rs, pw = totals(rnd)
        if not last:
            q = q + far_term(rnd)
        if i == 0:
            curvature = rw
            p, s = (r, w)
            z = q
        else:
            ratio = new / rr
            curvature = rw + ratio * (rs + pw) + ratio * ratio * curvature
            p = r + ratio * p
            s = w + ratio * s
            if not last:
                z = q + ratio * z
        rr = new
        step = rr / curvature
        x = x + step * p
        r = r - step * s
        if not last:
            w = w - step * z
    charges_out[...] = x
    residual_out[...] = r

    for rnd in range(ITERS):
        wait_all(fields.at[rnd, SELF, 0], field_send.at[rnd, SELF])

        @pl.when(clu < owners - 1)
        def _():
            wait_all(fields.at[rnd, BELOW], field_send.at[rnd, BELOW])

        @pl.when(clu > 0)
        def _():
            wait_all(fields.at[rnd, ABOVE], field_send.at[rnd, ABOVE])

    for rnd in range(ITERS + 1):
        wait_all(inbox.at[rnd, pl.ds(0, peers)], slab_send.at[rnd])


def shards(
    electronegativity,
    mm_potential,
    hardness,
    near_blocks,
    near_source,
    basis_in,
    far_coupling,
    far_source,
    far_target,
    far_count,
):
    clusters, atoms = hardness.shape
    owners = far_coupling.shape[1]
    width = far_coupling.shape[2] * basis_in.shape[1]
    vmem = pl.BlockSpec(memory_space=pltpu.VMEM)
    hbm = pl.BlockSpec(memory_space=pltpu.HBM)
    rounds = ITERS + 1
    arguments = (
        jnp.swapaxes(far_target, 1, 2),
        far_count,
        basis_in,
        electronegativity,
        mm_potential,
        far_coupling,
        near_blocks,
        jnp.swapaxes(near_source, 0, 1),
        hardness,
    )
    scalars = (0, 1, 7)
    held = [
        (pltpu.SMEM if i in scalars else pltpu.VMEM)(a.shape, a.dtype)
        for i, a in enumerate(arguments)
    ]
    return pl.pallas_call(
        functools.partial(kernel, owners),
        out_shape=(jax.ShapeDtypeStruct(hardness.shape, F32),) * 2,
        in_specs=[hbm] * len(arguments),
        out_specs=(vmem, vmem),
        scratch_shapes=held
        + [
            pltpu.VMEM((owners * width, atoms), BF16),
            pltpu.VMEM((owners * width, 2 * atoms), BF16),
            pltpu.VMEM((owners, clusters, width), F32),
            pltpu.VMEM((ITERS, 3, 2, clusters, atoms), F32),
            pltpu.VMEM((rounds, owners, 8, 128), F32),
            pltpu.VMEM((rounds, 2 * owners, 8, 128), F32),
            pltpu.SemaphoreType.DMA((len(arguments),)),
            pltpu.SemaphoreType.DMA((ITERS, 3)),
            pltpu.SemaphoreType.DMA((ITERS, 3)),
            pltpu.SemaphoreType.DMA((rounds,)),
            pltpu.SemaphoreType.DMA((rounds,)),
        ],
        compiler_params=pltpu.CompilerParams(
            collective_id=0, has_side_effects=True, vmem_limit_bytes=64 * 2**20
        ),
    )(*arguments)


def solution(mesh):
    placed = (
        P(("rep", "clu"), "sub"),
        P(("rep", "clu"), "sub"),
        P(("rep", "clu"), "sub"),
        P(("rep", "clu"), None, "sub", None),
        P(("rep", "clu"), None),
        P(("rep", "clu"), None, "sub"),
        P(("rep", "clu"), None, None, None),
        P(("rep", "clu"), None, None),
        P(("rep", "clu"), None, None),
        P(("rep", "clu"), None),
    )
    return jax.shard_map(
        shards,
        mesh=mesh,
        in_specs=placed,
        out_specs=(P(("rep", "clu"), "sub"), P(("rep", "clu"), "sub")),
        check_vma=False,
    )
```

```python
import functools

import jax
import jax.numpy as jnp
from jax import lax
from jax.experimental import pallas as pl
from jax.experimental.pallas import tpu as pltpu
from jax.sharding import PartitionSpec as P

ITERS = 3
MESH = pl.DeviceIdType.MESH
F32 = jnp.float32
BF16 = jnp.bfloat16
SELF, ABOVE, BELOW = 0, 1, 2


def each(first, count, body):
    if count - first <= 8:
        for i in range(first, count):
            body(i)
    else:
        lax.fori_loop(first, count, lambda i, _: (body(i), 0)[1], 0)


def halves(x):
    high = x.astype(BF16)
    low = (x - high.astype(F32)).astype(BF16)
    return high, low


def contract(a, b, dims):
    return lax.dot_general(a, b, (dims, ((), ())), preferred_element_type=F32)


def kernel(
    owners,
    *refs,
):
    arguments, refs = (refs[:9], refs[9:])
    results = refs[0]
    held, refs = (refs[1:10], refs[10:])
    target, count, basis, electro, potential, coupling, near, near_source, hardness_ref = held
    (
        picked_basis,
        expand,
        mask,
        fields,
        outbox,
        inbox,
        load_sem,
        field_send,
        field_recv,
        slab_send,
        slab_recv,
    ) = refs
    loads = [
        pltpu.make_async_copy(source, place, load_sem.at[i])
        for i, (source, place) in enumerate(zip(arguments, held))
    ]
    clusters, atoms = hardness_ref.shape
    slots = target.shape[1]
    rank = basis.shape[1]
    width = slots * rank
    group = 8
    groups = owners // group
    span = group * width
    peers = 2 * owners - 1
    clu = lax.axis_index("clu")
    sub = lax.axis_index("sub")
    mine = 2 * clu + sub

    def to_peers(act):
        def owner_step(o):
            d = lax.rem(clu + o, owners)
            act(d, 0)
            act(d, 1)

        act(clu, 1 - sub)
        each(1, owners, owner_step)

    barrier = pltpu.get_barrier_semaphore()
    to_peers(
        lambda d, t: pl.semaphore_signal(
            barrier, inc=1, device_id={"clu": d, "sub": t}, device_id_type=MESH
        )
    )

    for copy in loads:
        copy.start()

    row8 = lax.broadcasted_iota(jnp.int32, (clusters, 128), 0)
    slot_of_lane = lax.broadcasted_iota(jnp.int32, (clusters, width), 1) // rank

    def prepare(s):
        wanted = jnp.full((clusters, width), -1, jnp.int32)
        for k in range(slots):
            t = target[0, k, s]
            picked_basis[pl.ds((s * slots + k) * rank, rank), :] = basis[t]
            wanted = jnp.where(slot_of_lane == k, t, wanted)
        hit = (wanted == lax.broadcasted_iota(jnp.int32, (clusters, width), 0)) & (
            slot_of_lane < count[0, s]
        )
        mask[s] = jnp.where(hit, 1.0, 0.0)

    for copy in loads[:3]:
        copy.wait()
    each(0, owners, prepare)

    def send_field(rnd, v):
        fields[rnd, SELF, sub] = v
        source = fields.at[rnd, SELF, sub]

        def copy(kind, d, t):
            pltpu.make_async_remote_copy(
                src_ref=source,
                dst_ref=fields.at[rnd, kind, sub],
                send_sem=field_send.at[rnd, kind],
                recv_sem=field_recv.at[rnd, kind],
                device_id={"clu": d, "sub": t},
                device_id_type=MESH,
            ).start()

        copy(SELF, clu, 1 - sub)

        @pl.when(clu < owners - 1)
        def _():
            copy(BELOW, clu + 1, 0)
            copy(BELOW, clu + 1, 1)

        @pl.when(clu > 0)
        def _():
            copy(ABOVE, clu - 1, 0)
            copy(ABOVE, clu - 1, 1)

    def send_slabs(rnd, sums):
        def copy(d, t):
            pltpu.make_async_remote_copy(
                src_ref=outbox.at[rnd, d],
                dst_ref=inbox.at[rnd, mine],
                send_sem=slab_send.at[rnd],
                recv_sem=slab_recv.at[rnd],
                device_id={"clu": d, "sub": t},
                device_id_type=MESH,
            ).start()

        to_peers(copy)
        inbox[rnd, mine] = sums

    def fill_far(rnd, v, sums):
        parts = jnp.concatenate(halves(v), axis=0)

        def group_step(g):
            wide = contract(
                parts, picked_basis[pl.ds(pl.multiple_of(g * span, span), span), :], ((1,), (1,))
            )
            for j in range(group):
                piece = wide[:, j * width : (j + 1) * width]
                piece = (piece[:clusters] + piece[clusters:]) * mask[g * group + j]
                line = jnp.sum(piece, axis=0, keepdims=True)
                outbox[rnd, g * group + j] = jnp.where(row8 == 0, line, sums)

        each(0, groups, group_step)

    def send_sums(rnd, sums):
        each(0, owners, lambda d: outbox.__setitem__((rnd, d), sums))
        send_slabs(rnd, sums)

    def wait_all(ref, sem):
        pltpu.make_async_copy(ref, ref, sem).wait()

    def near_term(rnd):
        def whole(kind):
            return jnp.concatenate([fields[rnd, kind, 0], fields[rnd, kind, 1]], axis=1)

        def masked(value, c):
            return jnp.where(owner_row == c, value, jnp.zeros_like(value))

        def apply(total, inputs, blocks):
            for first, second in zip(blocks[::2], blocks[1::2]):
                left = jnp.concatenate([masked(inputs[n], c) for c, n in (first, second)], axis=0)
                right = jnp.concatenate([near[c, n] for c, n in (first, second)], axis=0)
                product = contract(left, right, ((1,), (1,)))
                total = product if total is None else total + product
            return total

        wait_all(fields.at[rnd, SELF, 0], field_recv.at[rnd, SELF])
        own = whole(SELF)
        inputs = [jnp.concatenate(halves(own), axis=0)]
        owner_row = lax.broadcasted_iota(jnp.int32, inputs[0].shape, 0) % clusters
        total = apply(None, inputs, [(c, 0) for c in range(clusters)])

        @pl.when(clu < owners - 1)
        def _():
            wait_all(fields.at[rnd, ABOVE], field_recv.at[rnd, ABOVE])

        @pl.when(clu > 0)
        def _():
            wait_all(fields.at[rnd, BELOW], field_recv.at[rnd, BELOW])

        above, below = (whole(ABOVE), whole(BELOW))
        for n in range(1, near.shape[1]):
            origin = origins[n]
            value = jnp.where(
                origin == here + clusters,
                above,
                jnp.where(origin == here - clusters, below, own),
            )
            inputs.append(jnp.concatenate(halves(value), axis=0))
        rest = [(c, n) for c in range(clusters) for n in range(1, near.shape[1])]
        total = apply(total, inputs, rest)
        size = 2 * clusters
        first, second = (total[:size, :atoms], total[size:, atoms:])
        both = first + second
        return both[:clusters] + both[clusters:]

    def receive(rnd):
        wait_all(inbox.at[rnd, pl.ds(0, peers)], slab_recv.at[rnd])

    def far_term(rnd):
        def group_step(g):
            lefts = []
            for j in range(group):
                s = g * group + j
                line = inbox[rnd, 2 * s, 0:1, :] + inbox[rnd, 2 * s + 1, 0:1, :]
                lefts.append(line * mask[s])
            left = jnp.concatenate(lefts, axis=1)
            left = jnp.concatenate(halves(left), axis=0)
            right = expand[pl.ds(pl.multiple_of(g * span, span), span), :]
            out = contract(left, right, ((1,), (0,)))
            out = out[:clusters] + out[clusters:]
            return out[:, :atoms] + out[:, atoms:]

        if groups == 1:
            return group_step(0)
        return lax.fori_loop(
            0, groups, lambda g, acc: acc + group_step(g), jnp.zeros((clusters, atoms), F32)
        )

    def totals(rnd):
        if owners <= 8:
            values = [inbox[rnd, i] for i in range(2 * owners)]
            while len(values) > 1:
                values = [a + b for a, b in zip(values[::2], values[1::2])]
            all_sums = values[0]
        else:
            all_sums = lax.fori_loop(
                0, 2 * owners, lambda i, acc: acc + inbox[rnd, i], jnp.zeros((8, 128), F32)
            )
        lane_sum = jnp.sum(all_sums, axis=1, keepdims=True)
        return [lane_sum[i : i + 1, :] for i in range(1, 5)]

    def pack(*pairs):
        out = jnp.zeros((8, 128), F32)
        for i, (a, b) in enumerate(pairs):
            out = jnp.where(row8 == i + 1, jnp.sum(a * b, axis=0, keepdims=True), out)
        return out

    def build_expand():
        row = lax.broadcasted_iota(jnp.int32, (width, width), 0)
        lane = lax.broadcasted_iota(jnp.int32, (width, width), 1)
        spread = jnp.where(row % rank == lane % rank, 1.0, 0.0).astype(BF16)
        per_chunk = width // rank
        same = row // rank == lane // rank

        def step(s):
            lines = coupling[0, s].astype(F32)
            folded = jnp.zeros((width, width), F32)
            for j in range(rank * rank // width):
                chunk = lines[:, j * width : (j + 1) * width]
                tall = jnp.broadcast_to(chunk[:, None, :], (slots, rank, width)).reshape(
                    width, width
                )
                folded = jnp.where(row % rank == lane // rank + j * per_chunk, tall, folded)
            tiled = contract(folded.astype(BF16), spread, ((1,), (0,)))
            diagonal = jnp.where(same, tiled, 0.0).astype(BF16)
            place = pl.ds(pl.multiple_of(s * width, width), width)
            high, low = halves(contract(diagonal, picked_basis[place, :], ((0,), (0,))))
            expand[place, 0:atoms] = high
            expand[place, atoms : 2 * atoms] = low

        each(0, owners, step)

    for copy in loads[3:5]:
        copy.wait()
    r = -(electro[...] + potential[...])
    x = jnp.zeros_like(r)
    empty = jnp.zeros((8, 128), F32)
    fill_far(0, r, empty)
    pl.semaphore_wait(barrier, peers)
    send_slabs(0, empty)
    send_field(0, r)
    loads[5].wait()
    build_expand()
    for copy in loads[6:]:
        copy.wait()
    hardness = hardness_ref[...]
    here = clu * clusters + lax.broadcasted_iota(jnp.int32, (clusters, 2 * atoms), 0)
    origins = []
    for n in range(near.shape[1]):
        origin = here
        for c in range(clusters):
            origin = jnp.where(here == clu * clusters + c, near_source[n, c], origin)
        origins.append(origin)
    w = hardness * r + near_term(0)
    receive(0)
    w = w + far_term(0)

    p, s, z, rr, curvature, step = (None,) * 6
    for i in range(ITERS):
        rnd = i + 1
        if i == 0:
            sums = pack((r, r), (r, w))
        else:
            sums = pack((r, r), (r, w), (r, s), (p, w))
        last = i == ITERS - 1
        if last:
            send_sums(rnd, sums)
            receive(rnd)
        else:
            fill_far(rnd, w, sums)
            send_slabs(rnd, jnp.where(row8 == 0, 0.0, sums))
            send_field(rnd, w)
            q = hardness * w + near_term(rnd)
            receive(rnd)
        new, rw, rs, pw = totals(rnd)
        if not last:
            q = q + far_term(rnd)
        if i == 0:
            curvature = rw
            p, s = (r, w)
            z = q
        else:
            ratio = new / rr
            curvature = rw + ratio * (rs + pw) + ratio * ratio * curvature
            p = r + ratio * p
            s = w + ratio * s
            if not last:
                z = q + ratio * z
        rr = new
        step = rr / curvature
        x = x + step * p
        r = r - step * s
        if not last:
            w = w - step * z
    results[0] = x
    results[1] = r

    for rnd in range(ITERS):
        wait_all(fields.at[rnd, SELF, 0], field_send.at[rnd, SELF])

        @pl.when(clu < owners - 1)
        def _():
            wait_all(fields.at[rnd, BELOW], field_send.at[rnd, BELOW])

        @pl.when(clu > 0)
        def _():
            wait_all(fields.at[rnd, ABOVE], field_send.at[rnd, ABOVE])

    for rnd in range(ITERS + 1):
        wait_all(inbox.at[rnd, pl.ds(0, peers)], slab_send.at[rnd])


def shards(
    electronegativity,
    mm_potential,
    hardness,
    near_blocks,
    near_source,
    basis_in,
    far_coupling,
    far_source,
    far_target,
    far_count,
):
    clusters, atoms = hardness.shape
    owners = far_coupling.shape[1]
    width = far_coupling.shape[2] * basis_in.shape[1]
    vmem = pl.BlockSpec(memory_space=pltpu.VMEM)
    hbm = pl.BlockSpec(memory_space=pltpu.HBM)
    rounds = ITERS + 1
    arguments = (
        jnp.swapaxes(far_target, 1, 2),
        far_count,
        basis_in,
        electronegativity,
        mm_potential,
        far_coupling,
        near_blocks,
        jnp.swapaxes(near_source, 0, 1),
        hardness,
    )
    scalars = (0, 1, 7)
    held = [
        (pltpu.SMEM if i in scalars else pltpu.VMEM)(a.shape, a.dtype)
        for i, a in enumerate(arguments)
    ]
    both = pl.pallas_call(
        functools.partial(kernel, owners),
        out_shape=jax.ShapeDtypeStruct((2,) + hardness.shape, F32),
        in_specs=[hbm] * len(arguments),
        out_specs=vmem,
        scratch_shapes=held
        + [
            pltpu.VMEM((owners * width, atoms), BF16),
            pltpu.VMEM((owners * width, 2 * atoms), BF16),
            pltpu.VMEM((owners, clusters, width), F32),
            pltpu.VMEM((ITERS, 3, 2, clusters, atoms), F32),
            pltpu.VMEM((rounds, owners, 8, 128), F32),
            pltpu.VMEM((rounds, 2 * owners, 8, 128), F32),
            pltpu.SemaphoreType.DMA((len(arguments),)),
            pltpu.SemaphoreType.DMA((ITERS, 3)),
            pltpu.SemaphoreType.DMA((ITERS, 3)),
            pltpu.SemaphoreType.DMA((rounds,)),
            pltpu.SemaphoreType.DMA((rounds,)),
        ],
        compiler_params=pltpu.CompilerParams(
            collective_id=0, has_side_effects=True, vmem_limit_bytes=64 * 2**20
        ),
    )(*arguments)
    return (both[0], both[1])


def solution(mesh):
    placed = (
        P(("rep", "clu"), "sub"),
        P(("rep", "clu"), "sub"),
        P(("rep", "clu"), "sub"),
        P(("rep", "clu"), None, "sub", None),
        P(("rep", "clu"), None),
        P(("rep", "clu"), None, "sub"),
        P(("rep", "clu"), None, None, None),
        P(("rep", "clu"), None, None),
        P(("rep", "clu"), None, None),
        P(("rep", "clu"), None),
    )
    return jax.shard_map(
        shards,
        mesh=mesh,
        in_specs=placed,
        out_specs=(P(("rep", "clu"), "sub"), P(("rep", "clu"), "sub")),
        check_vma=False,
    )
```

```python
import functools

import jax
import jax.numpy as jnp
from jax import lax
from jax.experimental import pallas as pl
from jax.experimental.pallas import tpu as pltpu
from jax.sharding import PartitionSpec as P

ITERS = 3
MESH = pl.DeviceIdType.MESH
F32 = jnp.float32
BF16 = jnp.bfloat16
SELF, ABOVE, BELOW = 0, 1, 2


def each(first, count, body):
    if count - first <= 8:
        for i in range(first, count):
            body(i)
    else:
        lax.fori_loop(first, count, lambda i, _: (body(i), 0)[1], 0)


def halves(x):
    high = x.astype(BF16)
    low = (x - high.astype(F32)).astype(BF16)
    return high, low


def contract(a, b, dims):
    return lax.dot_general(a, b, (dims, ((), ())), preferred_element_type=F32)


def kernel(
    owners,
    *refs,
):
    arguments, refs = (refs[:9], refs[9:])
    results = refs[0]
    held, refs = (refs[1:10], refs[10:])
    target, count, basis, electro, potential, coupling, near, near_source, hardness_ref = held
    (
        picked_basis,
        expand,
        mask,
        fields,
        outbox,
        inbox,
        load_sem,
        field_send,
        field_recv,
        slab_send,
        slab_recv,
    ) = refs
    loads = [
        pltpu.make_async_copy(source, place, load_sem.at[i])
        for i, (source, place) in enumerate(zip(arguments, held))
    ]
    clusters, atoms = hardness_ref.shape
    slots = target.shape[1]
    rank = basis.shape[1]
    width = slots * rank
    group = 8
    groups = owners // group
    span = group * width
    peers = 2 * owners - 1
    clu = lax.axis_index("clu")
    sub = lax.axis_index("sub")
    mine = 2 * clu + sub

    def to_peers(act):
        upper = lax.div(clu, owners // 2)

        def owner_step(i):
            rising = i + lax.div(i - clu + owners, owners)
            falling = owners - 1 - i
            falling = falling - lax.div(clu - falling + owners, owners)
            d = upper * rising + (1 - upper) * falling
            act(d, 0)
            act(d, 1)

        each(0, owners - 1, owner_step)
        act(clu, 1 - sub)

    barrier = pltpu.get_barrier_semaphore()
    to_peers(
        lambda d, t: pl.semaphore_signal(
            barrier, inc=1, device_id={"clu": d, "sub": t}, device_id_type=MESH
        )
    )

    for copy in loads:
        copy.start()

    row8 = lax.broadcasted_iota(jnp.int32, (clusters, 128), 0)
    slot_of_lane = lax.broadcasted_iota(jnp.int32, (clusters, width), 1) // rank

    def prepare(s):
        wanted = jnp.full((clusters, width), -1, jnp.int32)
        for k in range(slots):
            t = target[0, k, s]
            picked_basis[pl.ds((s * slots + k) * rank, rank), :] = basis[t]
            wanted = jnp.where(slot_of_lane == k, t, wanted)
        hit = (wanted == lax.broadcasted_iota(jnp.int32, (clusters, width), 0)) & (
            slot_of_lane < count[0, s]
        )
        mask[s] = jnp.where(hit, 1.0, 0.0)

    for copy in loads[:3]:
        copy.wait()
    each(0, owners, prepare)

    def send_field(rnd, v):
        fields[rnd, SELF, sub] = v
        source = fields.at[rnd, SELF, sub]

        def copy(kind, d, t):
            pltpu.make_async_remote_copy(
                src_ref=source,
                dst_ref=fields.at[rnd, kind, sub],
                send_sem=field_send.at[rnd, kind],
                recv_sem=field_recv.at[rnd, kind],
                device_id={"clu": d, "sub": t},
                device_id_type=MESH,
            ).start()

        copy(SELF, clu, 1 - sub)

        @pl.when(clu < owners - 1)
        def _():
            copy(BELOW, clu + 1, 0)
            copy(BELOW, clu + 1, 1)

        @pl.when(clu > 0)
        def _():
            copy(ABOVE, clu - 1, 0)
            copy(ABOVE, clu - 1, 1)

    def send_slabs(rnd, sums):
        def copy(d, t):
            pltpu.make_async_remote_copy(
                src_ref=outbox.at[rnd, d],
                dst_ref=inbox.at[rnd, mine],
                send_sem=slab_send.at[rnd],
                recv_sem=slab_recv.at[rnd],
                device_id={"clu": d, "sub": t},
                device_id_type=MESH,
            ).start()

        to_peers(copy)
        inbox[rnd, mine] = sums

    def fill_far(rnd, v, sums):
        parts = jnp.concatenate(halves(v), axis=0)

        def group_step(g):
            wide = contract(
                parts, picked_basis[pl.ds(pl.multiple_of(g * span, span), span), :], ((1,), (1,))
            )
            for j in range(group):
                piece = wide[:, j * width : (j + 1) * width]
                piece = (piece[:clusters] + piece[clusters:]) * mask[g * group + j]
                line = jnp.sum(piece, axis=0, keepdims=True)
                outbox[rnd, g * group + j] = jnp.where(row8 == 0, line, sums)

        each(0, groups, group_step)

    def send_sums(rnd, sums):
        each(0, owners, lambda d: outbox.__setitem__((rnd, d), sums))
        send_slabs(rnd, sums)

    def wait_all(ref, sem):
        pltpu.make_async_copy(ref, ref, sem).wait()

    def near_term(rnd):
        def whole(kind):
            return jnp.concatenate([fields[rnd, kind, 0], fields[rnd, kind, 1]], axis=1)

        def masked(value, c):
            return jnp.where(owner_row == c, value, jnp.zeros_like(value))

        def apply(total, inputs, blocks):
            for first, second in zip(blocks[::2], blocks[1::2]):
                left = jnp.concatenate([masked(inputs[n], c) for c, n in (first, second)], axis=0)
                right = jnp.concatenate([near[c, n] for c, n in (first, second)], axis=0)
                product = contract(left, right, ((1,), (1,)))
                total = product if total is None else total + product
            return total

        wait_all(fields.at[rnd, SELF, 0], field_recv.at[rnd, SELF])
        own = whole(SELF)
        inputs = [jnp.concatenate(halves(own), axis=0)]
        owner_row = lax.broadcasted_iota(jnp.int32, inputs[0].shape, 0) % clusters
        total = apply(None, inputs, [(c, 0) for c in range(clusters)])

        @pl.when(clu < owners - 1)
        def _():
            wait_all(fields.at[rnd, ABOVE], field_recv.at[rnd, ABOVE])

        @pl.when(clu > 0)
        def _():
            wait_all(fields.at[rnd, BELOW], field_recv.at[rnd, BELOW])

        above, below = (whole(ABOVE), whole(BELOW))
        for n in range(1, near.shape[1]):
            origin = origins[n]
            value = jnp.where(
                origin == here + clusters,
                above,
                jnp.where(origin == here - clusters, below, own),
            )
            inputs.append(jnp.concatenate(halves(value), axis=0))
        rest = [(c, n) for c in range(clusters) for n in range(1, near.shape[1])]
        total = apply(total, inputs, rest)
        size = 2 * clusters
        first, second = (total[:size, :atoms], total[size:, atoms:])
        both = first + second
        return both[:clusters] + both[clusters:]

    def receive(rnd):
        wait_all(inbox.at[rnd, pl.ds(0, peers)], slab_recv.at[rnd])

    def far_term(rnd):
        def group_step(g):
            lefts = []
            for j in range(group):
                s = g * group + j
                line = inbox[rnd, 2 * s, 0:1, :] + inbox[rnd, 2 * s + 1, 0:1, :]
                lefts.append(line * mask[s])
            left = jnp.concatenate(lefts, axis=1)
            left = jnp.concatenate(halves(left), axis=0)
            right = expand[pl.ds(pl.multiple_of(g * span, span), span), :]
            out = contract(left, right, ((1,), (0,)))
            out = out[:clusters] + out[clusters:]
            return out[:, :atoms] + out[:, atoms:]

        if groups == 1:
            return group_step(0)
        return lax.fori_loop(
            0, groups, lambda g, acc: acc + group_step(g), jnp.zeros((clusters, atoms), F32)
        )

    def totals(rnd):
        if owners <= 8:
            values = [inbox[rnd, i] for i in range(2 * owners)]
            while len(values) > 1:
                values = [a + b for a, b in zip(values[::2], values[1::2])]
            all_sums = values[0]
        else:
            all_sums = lax.fori_loop(
                0, 2 * owners, lambda i, acc: acc + inbox[rnd, i], jnp.zeros((8, 128), F32)
            )
        lane_sum = jnp.sum(all_sums, axis=1, keepdims=True)
        return [lane_sum[i : i + 1, :] for i in range(1, 5)]

    def pack(*pairs):
        out = jnp.zeros((8, 128), F32)
        for i, (a, b) in enumerate(pairs):
            out = jnp.where(row8 == i + 1, jnp.sum(a * b, axis=0, keepdims=True), out)
        return out

    def build_expand():
        row = lax.broadcasted_iota(jnp.int32, (width, width), 0)
        lane = lax.broadcasted_iota(jnp.int32, (width, width), 1)
        spread = jnp.where(row % rank == lane % rank, 1.0, 0.0).astype(BF16)
        per_chunk = width // rank
        same = row // rank == lane // rank

        def step(s):
            lines = coupling[0, s].astype(F32)
            folded = jnp.zeros((width, width), F32)
            for j in range(rank * rank // width):
                chunk = lines[:, j * width : (j + 1) * width]
                tall = jnp.broadcast_to(chunk[:, None, :], (slots, rank, width)).reshape(
                    width, width
                )
                folded = jnp.where(row % rank == lane // rank + j * per_chunk, tall, folded)
            tiled = contract(folded.astype(BF16), spread, ((1,), (0,)))
            diagonal = jnp.where(same, tiled, 0.0).astype(BF16)
            place = pl.ds(pl.multiple_of(s * width, width), width)
            high, low = halves(contract(diagonal, picked_basis[place, :], ((0,), (0,))))
            expand[place, 0:atoms] = high
            expand[place, atoms : 2 * atoms] = low

        each(0, owners, step)

    for copy in loads[3:5]:
        copy.wait()
    r = -(electro[...] + potential[...])
    x = jnp.zeros_like(r)
    empty = jnp.zeros((8, 128), F32)
    fill_far(0, r, empty)
    pl.semaphore_wait(barrier, peers)
    send_slabs(0, empty)
    send_field(0, r)
    loads[5].wait()
    build_expand()
    for copy in loads[6:]:
        copy.wait()
    hardness = hardness_ref[...]
    here = clu * clusters + lax.broadcasted_iota(jnp.int32, (clusters, 2 * atoms), 0)
    origins = []
    for n in range(near.shape[1]):
        origin = here
        for c in range(clusters):
            origin = jnp.where(here == clu * clusters + c, near_source[n, c], origin)
        origins.append(origin)
    w = hardness * r + near_term(0)
    receive(0)
    w = w + far_term(0)

    p, s, z, rr, curvature, step = (None,) * 6
    for i in range(ITERS):
        rnd = i + 1
        if i == 0:
            sums = pack((r, r), (r, w))
        else:
            sums = pack((r, r), (r, w), (r, s), (p, w))
        last = i == ITERS - 1
        if last:
            send_sums(rnd, sums)
            receive(rnd)
        else:
            fill_far(rnd, w, sums)
            send_slabs(rnd, jnp.where(row8 == 0, 0.0, sums))
            send_field(rnd, w)
            q = hardness * w + near_term(rnd)
            receive(rnd)
        new, rw, rs, pw = totals(rnd)
        if not last:
            q = q + far_term(rnd)
        if i == 0:
            curvature = rw
            p, s = (r, w)
            z = q
        else:
            ratio = new / rr
            curvature = rw + ratio * (rs + pw) + ratio * ratio * curvature
            p = r + ratio * p
            s = w + ratio * s
            if not last:
                z = q + ratio * z
        rr = new
        step = rr / curvature
        x = x + step * p
        r = r - step * s
        if not last:
            w = w - step * z
    results[0] = x
    results[1] = r

    for rnd in range(ITERS):
        wait_all(fields.at[rnd, SELF, 0], field_send.at[rnd, SELF])

        @pl.when(clu < owners - 1)
        def _():
            wait_all(fields.at[rnd, BELOW], field_send.at[rnd, BELOW])

        @pl.when(clu > 0)
        def _():
            wait_all(fields.at[rnd, ABOVE], field_send.at[rnd, ABOVE])

    for rnd in range(ITERS + 1):
        wait_all(inbox.at[rnd, pl.ds(0, peers)], slab_send.at[rnd])


def shards(
    electronegativity,
    mm_potential,
    hardness,
    near_blocks,
    near_source,
    basis_in,
    far_coupling,
    far_source,
    far_target,
    far_count,
):
    clusters, atoms = hardness.shape
    owners = far_coupling.shape[1]
    width = far_coupling.shape[2] * basis_in.shape[1]
    vmem = pl.BlockSpec(memory_space=pltpu.VMEM)
    hbm = pl.BlockSpec(memory_space=pltpu.HBM)
    rounds = ITERS + 1
    arguments = (
        jnp.swapaxes(far_target, 1, 2),
        far_count,
        basis_in,
        electronegativity,
        mm_potential,
        far_coupling,
        near_blocks,
        jnp.swapaxes(near_source, 0, 1),
        hardness,
    )
    scalars = (0, 1, 7)
    held = [
        (pltpu.SMEM if i in scalars else pltpu.VMEM)(a.shape, a.dtype)
        for i, a in enumerate(arguments)
    ]
    both = pl.pallas_call(
        functools.partial(kernel, owners),
        out_shape=jax.ShapeDtypeStruct((2,) + hardness.shape, F32),
        in_specs=[hbm] * len(arguments),
        out_specs=vmem,
        scratch_shapes=held
        + [
            pltpu.VMEM((owners * width, atoms), BF16),
            pltpu.VMEM((owners * width, 2 * atoms), BF16),
            pltpu.VMEM((owners, clusters, width), F32),
            pltpu.VMEM((ITERS, 3, 2, clusters, atoms), F32),
            pltpu.VMEM((rounds, owners, 8, 128), F32),
            pltpu.VMEM((rounds, 2 * owners, 8, 128), F32),
            pltpu.SemaphoreType.DMA((len(arguments),)),
            pltpu.SemaphoreType.DMA((ITERS, 3)),
            pltpu.SemaphoreType.DMA((ITERS, 3)),
            pltpu.SemaphoreType.DMA((rounds,)),
            pltpu.SemaphoreType.DMA((rounds,)),
        ],
        compiler_params=pltpu.CompilerParams(
            collective_id=0, has_side_effects=True, vmem_limit_bytes=64 * 2**20
        ),
    )(*arguments)
    return (both[0], both[1])


def solution(mesh):
    placed = (
        P(("rep", "clu"), "sub"),
        P(("rep", "clu"), "sub"),
        P(("rep", "clu"), "sub"),
        P(("rep", "clu"), None, "sub", None),
        P(("rep", "clu"), None),
        P(("rep", "clu"), None, "sub"),
        P(("rep", "clu"), None, None, None),
        P(("rep", "clu"), None, None),
        P(("rep", "clu"), None, None),
        P(("rep", "clu"), None),
    )
    return jax.shard_map(
        shards,
        mesh=mesh,
        in_specs=placed,
        out_specs=(P(("rep", "clu"), "sub"), P(("rep", "clu"), "sub")),
        check_vma=False,
    )
```
